512 devices in a mesh: seq: 64 (over z, y_hi, x), head: 8 (over y_lo, core).
Axes of the slice: x: 4, y: 8 (y_hi: 2, y_lo: 4; y = y_hi * 4 + y_lo), z: 8, core: 2. Of those that a mesh axis runs over, the one named last changes fastest.
Arguments:
- query_input: bfloat16 [57344, 4096], P(('seq', 'head')), may hold values from -12 to 12
- encoded_keys: bfloat16 [57344, 1024], P(('seq', 'head')), may hold values from -8 to 8
- input_values: bfloat16 [57344, 1024], P(('seq', 'head')), may hold values from -6 to 6
- sources: int32 [64, 3], P('seq'), may hold values from -1 to 62, as said below
Outputs:
- attended: bfloat16 [57344, 4096], P(('seq', 'head'))
The draws below stay inside these ranges and needn't reach their ends.
Inputs may be any that keep to these rules, and one draw needn't show every extreme that they name: `sources`: row c: column 0 is c - 1; columns 1 and 2 are c - 2**a and c - 2**b for two different a, b >= 1 with 2**a and 2**b below 64; an entry is -1 where that value is negative.
All inputs are finite; a program needn't handle non-finite values.
Results may differ from the reference program's by a relative error of at most 0.006.
Values may be sent and summed in bfloat16 or wider, within the bound.
No kernel may reach another device: no remote copies, remote signals or barrier semaphores. Data moves between devices by JAX's collectives and lax.ppermute only.
A program may use at most 64 MiB of HBM per device.

```python
from functools import reduce
import jax
import jax.numpy as jnp
from jax import lax

QUERY_HEADS = 32
KEY_VALUE_HEADS = 8
HEAD_SIZE = 128
SPAN_TOKENS = 896
SPAN_COUNT = 64
TOKEN_COUNT = 57344


def draw_query_input(key, part):
    key = jax.random.fold_in(key, 3)
    random_noise_key = jax.random.fold_in(key, 0)
    final_result = jnp.clip(2.5 * jax.random.normal(random_noise_key, (TOKEN_COUNT, QUERY_HEADS, HEAD_SIZE), jnp.float32), -10.0, 10.0)
    return final_result.reshape(TOKEN_COUNT, QUERY_HEADS * HEAD_SIZE).astype(jnp.bfloat16)


def draw_encoded_keys(key, part):
    key = jax.random.fold_in(key, 7)
    random_noise_key = jax.random.fold_in(key, 0)
    final_result = jnp.clip(jax.random.normal(random_noise_key, (TOKEN_COUNT, KEY_VALUE_HEADS, HEAD_SIZE), jnp.float32), -5.0, 5.0)
    return final_result.reshape(TOKEN_COUNT, KEY_VALUE_HEADS * HEAD_SIZE).astype(jnp.bfloat16)


def draw_sources(key, part):
    key = jax.random.fold_in(key, 5)
    distances = jnp.array([2 ** power for power in range(1, 31) if 2 ** power < SPAN_COUNT], jnp.int32)
    amount = distances.shape[0]
    first_key, second_key = jax.random.split(key)
    row_index = jnp.arange(SPAN_COUNT, dtype=jnp.int32)
    first_pick = jax.random.randint(first_key, (SPAN_COUNT,), 0, amount)
    forced = SPAN_COUNT - 1 - row_index
    first_pick = jnp.where(forced < amount, forced, first_pick)
    second_pick = (first_pick + jax.random.randint(second_key, (SPAN_COUNT,), 1, amount)) % amount
    table = jnp.stack([row_index - 1, row_index - distances[first_pick], row_index - distances[second_pick]], 1)
    return jnp.where(table >= 0, table, -1).astype(jnp.int32)


def block_levels(rng, dims, cuts, smallest, top_value):
    loudness = 1.0
    for dim, parts in cuts:
        steps = jax.random.uniform(jax.random.fold_in(jax.random.fold_in(rng, 6), dim), (parts,), jnp.float32, smallest / len(cuts), top_value / len(cuts))
        loudness = loudness * jnp.repeat(jnp.exp(steps), dims[dim] // parts).reshape((-1,) + (1,) * (len(dims) - 1 - dim))
    return loudness


def bell_draw(stream_key, dims, scale, limit, pieces=(), kind=jnp.bfloat16):
    loudness = block_levels(stream_key, dims, pieces, -0.22, 0.18) if pieces else 1.0
    entries = jax.random.normal(stream_key, dims, jnp.float32) * scale * loudness
    return jnp.minimum(jnp.maximum(entries, -limit), limit).astype(kind)


def setup_inputs(seed: int = 0) -> dict:
    keys = jax.random.split(jax.random.key(seed), 5)
    query_input = draw_query_input(jax.random.fold_in(keys[4], 71), 0)
    encoded_keys = draw_encoded_keys(jax.random.fold_in(keys[4], 71), 0)
    input_values = bell_draw(keys[2], (TOKEN_COUNT, KEY_VALUE_HEADS * HEAD_SIZE), 1.0, 6.0, ((0, 512),))
    sources = draw_sources(jax.random.fold_in(keys[4], 71), 0)
    return {"query_input": query_input, "encoded_keys": encoded_keys, "input_values": input_values, "sources": sources}


negative_fill = -1e30


def block_terms(query_rows, key_rows, value_rows, causal):
    scores = jnp.einsum("qhd,khd->hqk", query_rows.astype(jnp.float32), key_rows.astype(jnp.float32)) * (HEAD_SIZE ** -0.5)
    if causal:
        position = jnp.arange(query_rows.shape[0])
        allowed = position[:, None] >= position[None, :]
        scores = jnp.where(allowed[None], scores, negative_fill)
    highest = jnp.max(scores, axis=-1)
    weights = jnp.exp(scores - highest[..., None]).astype(jnp.bfloat16)
    row_total = jnp.sum(weights.astype(jnp.float32), axis=-1)
    partial_out = jnp.einsum("hqk,khd->hqd", weights.astype(jnp.float32), value_rows.astype(jnp.float32))
    return highest, row_total, partial_out


def combine(block_list, validity):
    maxima = [jnp.where(is_valid, block_term[0], negative_fill) for block_term, is_valid in zip(block_list, validity)]
    overall = reduce(jnp.maximum, maxima)
    weighted = jnp.zeros(block_list[0][2].shape, jnp.float32)
    normalizer = jnp.zeros(block_list[0][1].shape, jnp.float32)
    for block_term, is_valid in zip(block_list, validity):
        factor = jnp.where(is_valid, jnp.exp(block_term[0] - overall), 0.0)
        weighted = weighted + factor[..., None] * block_term[2]
        normalizer = normalizer + factor * block_term[1]
    return weighted / normalizer[..., None]


def reference(query_input, encoded_keys, input_values, sources):
    group_width = QUERY_HEADS // KEY_VALUE_HEADS
    query_all = query_input.reshape(SPAN_COUNT, SPAN_TOKENS, QUERY_HEADS, HEAD_SIZE)
    keys_combined = encoded_keys.reshape(SPAN_COUNT, SPAN_TOKENS, KEY_VALUE_HEADS, HEAD_SIZE)
    values_combined = input_values.reshape(SPAN_COUNT, SPAN_TOKENS, KEY_VALUE_HEADS, HEAD_SIZE)

    def expand(array_part):
        return jnp.repeat(array_part, group_width, axis=1)

    def one_span(span_index):
        query_rows = query_all[span_index]
        block_list = [block_terms(query_rows, expand(keys_combined[span_index]), expand(values_combined[span_index]), True)]
        validity = [jnp.array(True)]
        for column in range(3):
            source = sources[span_index, column]
            clamped = jnp.maximum(source, 0).astype(jnp.int32)
            block_list.append(block_terms(query_rows, expand(keys_combined[clamped]), expand(values_combined[clamped]), False))
            validity.append(source >= 0)
        final_result = combine(block_list, validity)
        return jnp.transpose(final_result, (1, 0, 2)).reshape(SPAN_TOKENS, QUERY_HEADS * HEAD_SIZE).astype(jnp.bfloat16)

    return lax.map(one_span, jnp.arange(SPAN_COUNT, dtype=jnp.int32)).reshape(TOKEN_COUNT, QUERY_HEADS * HEAD_SIZE)
```

```python
import functools

import jax
import jax.numpy as jnp
import numpy as np
from jax import lax
from jax.experimental import pallas as pl
from jax.experimental.pallas import tpu as pltpu
from jax.sharding import PartitionSpec as P

HEAD_SIZE = 128
AXES = ("seq", "head")
SPANS, SLOTS, HALF, COLUMN = 64, 8, 4, 4
LOG_SCALE = float(HEAD_SIZE**-0.5 * np.log2(np.e))
EMPTY = -1e30
F32, BF16 = jnp.float32, jnp.bfloat16


def slot_order(span):
    if (span // COLUMN) % 2 == 0:
        return list(range(SLOTS))
    return [(SLOTS // 2 - 1 - slot // 2) * 2 + slot % 2 for slot in range(SLOTS)]


def exchange(value):
    groups = [[span * SLOTS + slot for slot in slot_order(span)] for span in range(SPANS)]
    return lax.all_to_all(
        value, AXES, split_axis=0, concat_axis=0, tiled=True, axis_index_groups=groups
    )


def moved(value, target):
    pairs = []
    for span in range(SPANS):
        goal = target(span)
        if goal is not None:
            here, there = slot_order(span), slot_order(goal)
            pairs += [(span * SLOTS + a, goal * SLOTS + b) for a, b in zip(here, there)]
    return lax.ppermute(value, AXES, pairs)


def ahead(distance):
    return lambda span: span + distance if span + distance < SPANS else None


def along_row(distance):
    return lambda span: span // COLUMN * COLUMN + (span + distance) % COLUMN


def scores_of(query, key):
    return lax.dot_general(query, key, (((1,), (1,)), ((), ())), preferred_element_type=F32)


def block_step(q_ref, key_ref, value_ref, top_ref, total_ref, part_ref, rows_each):
    heads = q_ref.shape[1] // HEAD_SIZE

    def rows_step(tile, _):
        rows = pl.ds(pl.multiple_of(tile * rows_each, rows_each), rows_each)

        def score(head):
            return scores_of(q_ref[rows, pl.ds(head * HEAD_SIZE, HEAD_SIZE)], key_ref[...])

        following = score(0)
        for head in range(heads):
            scores = following
            if head + 1 < heads:
                following = score(head + 1)
            lanes = pl.ds(head * HEAD_SIZE, HEAD_SIZE)
            old_top = top_ref[rows, lanes]
            top = jnp.maximum(old_top, jnp.max(scores, axis=1, keepdims=True) * LOG_SCALE)
            weights = jnp.exp2(scores * LOG_SCALE - top[:, :1]).astype(BF16)
            sums = jnp.dot(weights, value_ref[...], preferred_element_type=F32)
            factor = jnp.exp2(old_top - top)
            top_ref[rows, lanes] = top
            part_ref[rows, lanes] = part_ref[rows, lanes] * factor + sums[:, :HEAD_SIZE]
            total_ref[rows, lanes] = total_ref[rows, lanes] * factor + sums[:, HEAD_SIZE:]
        return 0

    lax.fori_loop(0, q_ref.shape[0] // rows_each, rows_step, 0)


def own_kernel(place_ref, q_ref, key_ref, value_ref, top_ref, total_ref, part_ref, wide_ref):
    mirrored = place_ref[0]
    tokens = q_ref.shape[0]
    heads = q_ref.shape[1] // HEAD_SIZE
    chunk = tokens // HALF
    wide_ref[:, :HEAD_SIZE] = value_ref[...]
    wide_ref[:, HEAD_SIZE:] = jnp.ones((tokens, HEAD_SIZE), BF16)
    order = lax.broadcasted_iota(jnp.int32, (chunk, chunk), 0)
    allowed = order >= lax.broadcasted_iota(jnp.int32, (chunk, chunk), 1)
    for turn in range(HALF):
        start = jnp.where(mirrored == 1, (HALF - 1 - turn) * chunk, turn * chunk)
        rows = pl.ds(pl.multiple_of(start, chunk), chunk)
        if turn:
            earlier = jnp.where(mirrored == 1, (HALF - turn) * chunk, 0)
            before = pl.ds(pl.multiple_of(earlier, chunk), turn * chunk)
        for head in range(heads):
            lanes = pl.ds(head * HEAD_SIZE, HEAD_SIZE)
            query = q_ref[rows, lanes]
            near = jnp.where(allowed, scores_of(query, key_ref[rows, :]), EMPTY)
            top = jnp.max(near, axis=1, keepdims=True)
            if turn:
                far = scores_of(query, key_ref[before, :])
                top = jnp.maximum(top, jnp.max(far, axis=1, keepdims=True))
            top = top * LOG_SCALE
            weights = jnp.exp2(near * LOG_SCALE - top).astype(BF16)
            sums = jnp.dot(weights, wide_ref[rows, :], preferred_element_type=F32)
            if turn:
                weights = jnp.exp2(far * LOG_SCALE - top).astype(BF16)
                sums += jnp.dot(weights, wide_ref[before, :], preferred_element_type=F32)
            top_ref[rows, lanes] = jnp.broadcast_to(top, (chunk, HEAD_SIZE))
            part_ref[rows, lanes] = sums[:, :HEAD_SIZE]
            total_ref[rows, lanes] = sums[:, HEAD_SIZE:]


def earlier_kernel(use_ref, q_ref, *refs, blocks, last):
    pairs, refs = refs[: 2 * blocks], refs[2 * blocks :]
    old, refs = refs[:3], refs[3:]
    if last:
        out_ref, top_ref, total_ref, part_ref, wide_ref, key_buffer = refs
    else:
        top_ref, total_ref, part_ref, wide_ref, key_buffer = refs
    tokens = q_ref.shape[0]
    for new_ref, old_ref in zip((top_ref, total_ref, part_ref), old):
        new_ref[...] = old_ref[...]
    wide_ref[:, HEAD_SIZE:] = jnp.ones((tokens, HEAD_SIZE), BF16)

    def one(block, _):
        @pl.when(use_ref[block] == 1)
        def _():
            for number in range(blocks):

                @pl.when(block == number)
                def _():
                    key_buffer[...] = pairs[2 * number][...]
                    wide_ref[:, :HEAD_SIZE] = pairs[2 * number + 1][...]

            block_step(q_ref, key_buffer, wide_ref, top_ref, total_ref, part_ref, tokens // HALF)

        return 0

    lax.fori_loop(0, blocks, one, 0)
    if last:
        out_ref[...] = (part_ref[...] / total_ref[...]).astype(BF16)


VMEM = pl.BlockSpec(memory_space=pltpu.VMEM)
SMEM = pl.BlockSpec(memory_space=pltpu.SMEM)
PARAMS = dict(vmem_limit_bytes=40 * 2**20)


def own_call(place, query, key, value):
    running = jax.ShapeDtypeStruct(query.shape, F32)
    wide = pltpu.VMEM((key.shape[0], 2 * HEAD_SIZE), BF16)
    return pl.pallas_call(
        own_kernel,
        out_shape=[running] * 3,
        in_specs=[SMEM, VMEM, VMEM, VMEM],
        out_specs=[VMEM] * 3,
        scratch_shapes=[wide],
        compiler_params=pltpu.CompilerParams(**PARAMS),
    )(place, query, key, value)


def earlier_call(use, query, blocks, state, last):
    running = [jax.ShapeDtypeStruct(query.shape, F32)] * 3
    scratch = [
        pltpu.VMEM((query.shape[0], 2 * HEAD_SIZE), BF16),
        pltpu.VMEM((query.shape[0], HEAD_SIZE), BF16),
    ]
    if last:
        scratch = [pltpu.VMEM(query.shape, F32)] * 3 + scratch
    arrays = [part for block in blocks for part in block]
    return pl.pallas_call(
        functools.partial(earlier_kernel, blocks=len(blocks), last=last),
        out_shape=jax.ShapeDtypeStruct(query.shape, BF16) if last else running,
        in_specs=[SMEM] + [VMEM] * (1 + len(arrays) + 3),
        out_specs=VMEM if last else [VMEM] * 3,
        scratch_shapes=scratch,
        compiler_params=pltpu.CompilerParams(**PARAMS),
    )(use, query, *arrays, *state)


def per_device(query_input, encoded_keys, input_values, sources):
    tokens = query_input.shape[0]
    span = lax.axis_index("seq")
    column = span % COLUMN
    mirrored = (span // COLUMN) % 2

    def gathered(value):
        cut = value.reshape(tokens, SLOTS, -1).transpose(1, 0, 2)
        return exchange(cut).reshape(tokens * SLOTS, -1)

    key = gathered(encoded_keys)
    value = gathered(input_values)
    query = gathered(query_input)

    def fetched(part):
        half = moved(part, ahead(4))
        eight = moved(part, ahead(8))
        far = moved(part, ahead(32))
        one = moved(jnp.where(column >= 3, half, part), along_row(1))
        two = moved(jnp.where(column >= 2, half, part), along_row(2))
        sixteen = moved(eight, ahead(8))
        return {1: one, 2: two, 4: half, 8: eight, 16: sixteen, 32: far}

    keys, values = fetched(key), fetched(value)
    row = sources[0]

    def wanted(distance):
        if distance == 1:
            return row[0] >= 0
        return jnp.any((row[1:] >= 0) & (span - row[1:] == distance))

    def use(distances):
        return jnp.stack([wanted(d) for d in distances]).astype(jnp.int32)

    state = own_call(mirrored.reshape(1).astype(jnp.int32), query, key, value)
    early, late = (8, 4, 16), (1, 2, 32)
    state = earlier_call(use(early), query, [(keys[d], values[d]) for d in early], state, False)
    attended = earlier_call(use(late), query, [(keys[d], values[d]) for d in late], state, True)
    back = exchange(attended.reshape(SLOTS, tokens, -1))
    return back.transpose(1, 0, 2).reshape(tokens, -1)


def solution(mesh):
    in_specs = (P(AXES, None), P(AXES, None), P(AXES, None), P("seq", None))
    return jax.shard_map(
        per_device, mesh=mesh, in_specs=in_specs, out_specs=P(AXES, None), check_vma=False
    )
```

```python
import functools

import jax
import jax.numpy as jnp
import numpy as np
from jax import lax
from jax.experimental import pallas as pl
from jax.experimental.pallas import tpu as pltpu
from jax.sharding import PartitionSpec as P

HEAD_SIZE = 128
AXES = ("seq", "head")
SPANS, SLOTS, HALF, COLUMN = 64, 8, 4, 4
LOG_SCALE = float(HEAD_SIZE**-0.5 * np.log2(np.e))
EMPTY = -1e30
F32, BF16 = jnp.float32, jnp.bfloat16


def slot_order(span):
    if (span // COLUMN) % 2 == 0:
        return list(range(SLOTS))
    return [(SLOTS // 2 - 1 - slot // 2) * 2 + slot % 2 for slot in range(SLOTS)]


def exchange(value):
    groups = [[span * SLOTS + slot for slot in slot_order(span)] for span in range(SPANS)]
    return lax.all_to_all(
        value, AXES, split_axis=0, concat_axis=0, tiled=True, axis_index_groups=groups
    )


def moved(value, target):
    pairs = []
    for span in range(SPANS):
        goal = target(span)
        if goal is not None:
            here, there = slot_order(span), slot_order(goal)
            pairs += [(span * SLOTS + a, goal * SLOTS + b) for a, b in zip(here, there)]
    return lax.ppermute(value, AXES, pairs)


def ahead(distance):
    return lambda span: span + distance if span + distance < SPANS else None


def along_row(distance):
    return lambda span: span // COLUMN * COLUMN + (span + distance) % COLUMN


def scores_of(query, key):
    return lax.dot_general(query, key, (((1,), (1,)), ((), ())), preferred_element_type=F32)


def block_step(q_ref, key_ref, wide_ref, state):
    top_ref, total_ref, part_ref = state
    heads = q_ref.shape[1] // HEAD_SIZE
    half = q_ref.shape[0] // 2

    def rows_step(tile, _):
        rows = pl.ds(pl.multiple_of(tile * half, half), half)

        def score(head):
            return scores_of(q_ref[rows, pl.ds(head * HEAD_SIZE, HEAD_SIZE)], key_ref[...])

        following = score(0)
        for head in range(heads):
            scores = following
            if head + 1 < heads:
                following = score(head + 1)
            lanes = pl.ds(head * HEAD_SIZE, HEAD_SIZE)
            old_top = top_ref[rows, lanes]
            top = jnp.maximum(old_top, jnp.max(scores, axis=1, keepdims=True) * LOG_SCALE)
            weights = jnp.exp2(scores * LOG_SCALE - top[:, :1]).astype(BF16)
            sums = jnp.dot(weights, wide_ref[...], preferred_element_type=F32)
            factor = jnp.exp2(old_top - top)
            top_ref[rows, lanes] = top
            part_ref[rows, lanes] = part_ref[rows, lanes] * factor + sums[:, :HEAD_SIZE]
            total_ref[rows, lanes] = total_ref[rows, lanes] * factor + sums[:, HEAD_SIZE:]
        return 0

    lax.fori_loop(0, 2, rows_step, 0)


def causal_step(mirrored, q_ref, key_ref, wide_ref, state):
    top_ref, total_ref, part_ref = state
    tokens = q_ref.shape[0]
    heads = q_ref.shape[1] // HEAD_SIZE
    chunk = tokens // HALF
    order = lax.broadcasted_iota(jnp.int32, (chunk, chunk), 0)
    allowed = order >= lax.broadcasted_iota(jnp.int32, (chunk, chunk), 1)
    for turn in range(HALF):
        start = jnp.where(mirrored == 1, (HALF - 1 - turn) * chunk, turn * chunk)
        rows = pl.ds(pl.multiple_of(start, chunk), chunk)
        if turn:
            earlier = jnp.where(mirrored == 1, (HALF - turn) * chunk, 0)
            before = pl.ds(pl.multiple_of(earlier, chunk), turn * chunk)
        for head in range(heads):
            lanes = pl.ds(head * HEAD_SIZE, HEAD_SIZE)
            query = q_ref[rows, lanes]
            near = jnp.where(allowed, scores_of(query, key_ref[rows, :]), EMPTY)
            top = jnp.max(near, axis=1, keepdims=True)
            if turn:
                far = scores_of(query, key_ref[before, :])
                top = jnp.maximum(top, jnp.max(far, axis=1, keepdims=True))
            top = top * LOG_SCALE
            weights = jnp.exp2(near * LOG_SCALE - top).astype(BF16)
            sums = jnp.dot(weights, wide_ref[rows, :], preferred_element_type=F32)
            if turn:
                weights = jnp.exp2(far * LOG_SCALE - top).astype(BF16)
                sums += jnp.dot(weights, wide_ref[before, :], preferred_element_type=F32)
            top_ref[rows, lanes] = jnp.broadcast_to(top, (chunk, HEAD_SIZE))
            part_ref[rows, lanes] = sums[:, :HEAD_SIZE]
            total_ref[rows, lanes] = sums[:, HEAD_SIZE:]


def start_sources(plan_ref, sources, buffer, sem):
    tokens = buffer.shape[0] // 3
    slot = jnp.int32(0)
    for column in range(3):
        here = jnp.bool_(False)
        for kind, pieces in sources.items():
            chosen = plan_ref[column] == kind
            here = here | chosen

            @pl.when(chosen)
            def _():
                begin = 0
                for number, ref in enumerate(pieces):
                    rows = pl.ds(pl.multiple_of(slot * tokens, tokens) + begin, ref.shape[0])
                    pltpu.make_async_copy(ref, buffer.at[rows], sem).start()
                    begin += ref.shape[0]

        slot = slot + here.astype(jnp.int32)
    return slot


def earlier_blocks(found, q_ref, wide_ref, buffer, sem, state):
    tokens = buffer.shape[0] // 3
    for number in (1, 2, 3):

        @pl.when(found == number)
        def _():
            here = buffer.at[pl.ds(0, number * tokens)]
            pltpu.make_async_copy(here, here, sem).wait()

    def add(rows):
        here, wide = buffer.at[rows], wide_ref.at[pl.ds(0, rows.size)]
        wide[:, :HEAD_SIZE] = here[:, HEAD_SIZE:]
        block_step(q_ref, here.at[:, pl.ds(0, HEAD_SIZE)], wide, state)

    pl.when(found >= 2)(lambda: add(pl.ds(0, 2 * tokens)))
    odd = pl.multiple_of((found // 2) * 2 * tokens, tokens)
    pl.when(found % 2 == 1)(lambda: add(pl.ds(odd, tokens)))


def attend_kernel(plan_ref, q_ref, *refs, pieces, first, last):
    refs = list(refs)

    def take(count):
        taken, refs[:] = refs[:count], refs[count:]
        return taken

    own_ref = take(1)[0] if first else None
    sources = {kind: take(count) for kind, count in pieces}
    old = [] if first else take(2)
    if last:
        (out_ref,) = take(1)
        (new_part,) = take(1)
    else:
        rows_out, new_part = take(2)
    top_ref, total_ref, wide_ref, buffer, sem = take(5)
    state = (top_ref, total_ref, new_part)
    found = start_sources(plan_ref, sources, buffer, sem)
    wide_ref[:, HEAD_SIZE:] = jnp.ones((wide_ref.shape[0], HEAD_SIZE), BF16)
    if first:
        wide = wide_ref.at[pl.ds(0, own_ref.shape[0])]
        wide[:, :HEAD_SIZE] = own_ref[:, HEAD_SIZE:]
        causal_step(plan_ref[3], q_ref, own_ref.at[:, pl.ds(0, HEAD_SIZE)], wide, state)
    else:
        rows_buffer, part_buffer, old_sem = refs
        copies = [
            pltpu.make_async_copy(old[0], rows_buffer, old_sem.at[0]),
            pltpu.make_async_copy(old[1], part_buffer, old_sem.at[1]),
        ]
        for copy in copies:
            copy.start()
        top_ref[...] = jnp.full(top_ref.shape, EMPTY, F32)
        total_ref[...] = jnp.zeros(total_ref.shape, F32)
        new_part[...] = jnp.zeros(new_part.shape, F32)
    earlier_blocks(found, q_ref, wide_ref, buffer, sem, state)
    if not first:
        for copy in copies:
            copy.wait()
    heads = q_ref.shape[1] // HEAD_SIZE
    packed = jnp.zeros((q_ref.shape[0], HEAD_SIZE), F32)
    lane = lax.broadcasted_iota(jnp.int32, packed.shape, 1)
    for head in range(heads):
        lanes = pl.ds(head * HEAD_SIZE, HEAD_SIZE)
        top, total = top_ref[:, lanes], total_ref[:, lanes]
        if not first:
            old_top = rows_buffer[:, head : head + 1]
            old_total = rows_buffer[:, heads + head : heads + head + 1]
            both_top = jnp.maximum(old_top, top)
            before, now = jnp.exp2(old_top - both_top), jnp.exp2(top - both_top)
            top, total = both_top, old_total * before + total * now
            part = part_buffer[:, lanes] * before + new_part[:, lanes] * now
            if last:
                out_ref[:, lanes] = (part / total).astype(BF16)
            else:
                new_part[:, lanes] = part
        if not last:
            packed = jnp.where(lane == head, top, packed)
            packed = jnp.where(lane == heads + head, total, packed)
    if not last:
        rows_out[...] = packed


VMEM = pl.BlockSpec(memory_space=pltpu.VMEM)
SMEM = pl.BlockSpec(memory_space=pltpu.SMEM)
ANY = pl.BlockSpec(memory_space=pl.ANY)
PARAMS = dict(vmem_limit_bytes=40 * 2**20)


def attend(plan, query, blocks, own=None, state=None, last=False):
    tokens = query.shape[0]
    first = own is not None
    running, packed = (query.shape, F32), ((tokens, HEAD_SIZE), F32)
    result = [(query.shape, BF16)] if last else [packed, running]
    pieces = [piece for kind in blocks for piece in blocks[kind]]
    scratch = [pltpu.VMEM(*running)] * (3 if last else 2) + [
        pltpu.VMEM((2 * tokens, 2 * HEAD_SIZE), BF16),
        pltpu.VMEM((3 * tokens, 2 * HEAD_SIZE), BF16),
        pltpu.SemaphoreType.DMA,
    ]
    if not first:
        scratch += [pltpu.VMEM(*packed), pltpu.VMEM(*running), pltpu.SemaphoreType.DMA((2,))]
    counts = tuple((kind, len(blocks[kind])) for kind in blocks)
    found = pl.pallas_call(
        functools.partial(attend_kernel, pieces=counts, first=first, last=last),
        out_shape=[jax.ShapeDtypeStruct(*kind) for kind in result],
        in_specs=[SMEM, VMEM] + [VMEM] * first + [ANY] * (len(pieces) + 2 * (not first)),
        out_specs=[VMEM] * len(result),
        scratch_shapes=scratch,
        compiler_params=pltpu.CompilerParams(**PARAMS),
    )(plan, query, *([own] if first else []), *pieces, *([] if first else state))
    return found[0] if last else found


CALLS = ((4, 8, 1), (2, 16, 32))


def per_device(query_input, encoded_keys, input_values, sources):
    tokens = query_input.shape[0]
    span = lax.axis_index("seq")
    column = span % COLUMN
    mirrored = (span // COLUMN) % 2

    plan = jnp.where(sources[0] >= 0, span - sources[0], 0).astype(jnp.int32)
    plan = jnp.concatenate([plan, mirrored[None].astype(jnp.int32)])

    def slots(value):
        return value.reshape(tokens, SLOTS, -1)

    both = jnp.concatenate([slots(encoded_keys), slots(input_values)], 2).transpose(1, 0, 2)
    own = exchange(both).reshape(-1, 2 * HEAD_SIZE)
    query_cut = slots(query_input).transpose(1, 0, 2)
    four = moved(own, ahead(4))
    eight = moved(own, ahead(8))
    query = exchange(query_cut).reshape(tokens * SLOTS, -1)
    late, eight = lax.optimization_barrier((own, eight))
    blocks = {
        1: moved(jnp.where(column >= 3, four, own), along_row(1)),
        2: moved(jnp.where(column >= 2, four, own), along_row(2)),
        4: four,
        8: eight,
        16: moved(eight, ahead(8)),
        32: moved(late, ahead(32)),
    }
    blocks = {kind: [blocks[kind]] for kind in blocks}
    state = None
    for number, kinds in enumerate(CALLS):
        state = attend(
            plan,
            query,
            {kind: blocks[kind] for kind in kinds},
            own=own if number == 0 else None,
            state=state,
            last=number == len(CALLS) - 1,
        )
    back = exchange(state.reshape(SLOTS, tokens, -1))
    return back.transpose(1, 0, 2).reshape(tokens, -1)


def solution(mesh):
    in_specs = (P(AXES, None), P(AXES, None), P(AXES, None), P("seq", None))
    return jax.shard_map(
        per_device, mesh=mesh, in_specs=in_specs, out_specs=P(AXES, None), check_vma=False
    )
```

```python
import functools

import jax
import jax.numpy as jnp
import numpy as np
from jax import lax
from jax.experimental import pallas as pl
from jax.experimental.pallas import tpu as pltpu
from jax.sharding import PartitionSpec as P

HEAD_SIZE = 128
AXES = ("seq", "head")
SPANS, SLOTS, HALF, COLUMN, PLANE = 64, 8, 4, 4, 8
LOG_SCALE = float(HEAD_SIZE**-0.5 * np.log2(np.e))
EMPTY = -1e30
F32, BF16 = jnp.float32, jnp.bfloat16


def slot_order(span):
    if (span // COLUMN) % 2 == 0:
        return list(range(SLOTS))
    return [(SLOTS // 2 - 1 - slot // 2) * 2 + slot % 2 for slot in range(SLOTS)]


def exchange(value):
    groups = [[span * SLOTS + slot for slot in slot_order(span)] for span in range(SPANS)]
    return lax.all_to_all(
        value, AXES, split_axis=0, concat_axis=0, tiled=True, axis_index_groups=groups
    )


def moved(value, target):
    pairs = []
    for span in range(SPANS):
        goal = target(span)
        if goal is not None:
            here, there = slot_order(span), slot_order(goal)
            pairs += [(span * SLOTS + a, goal * SLOTS + b) for a, b in zip(here, there)]
    return lax.ppermute(value, AXES, pairs)


def ahead(distance):
    return lambda span: span + distance if span + distance < SPANS else None


def along_row(distance):
    return lambda span: span // COLUMN * COLUMN + (span + distance) % COLUMN


def behind(*planes):
    count = SPANS // PLANE

    def target(span):
        plane = span // PLANE
        return (plane - 2) % count * PLANE + span % PLANE if plane in planes else None

    return target


def scores_of(query, key):
    return lax.dot_general(query, key, (((1,), (1,)), ((), ())), preferred_element_type=F32)


def block_step(q_ref, key_ref, wide_ref, state):
    top_ref, total_ref, part_ref = state
    heads = q_ref.shape[1] // HEAD_SIZE
    half = q_ref.shape[0] // 2

    def rows_step(tile, _):
        rows = pl.ds(pl.multiple_of(tile * half, half), half)

        def score(head):
            return scores_of(q_ref[rows, pl.ds(head * HEAD_SIZE, HEAD_SIZE)], key_ref[...])

        following = score(0)
        for head in range(heads):
            scores = following
            if head + 1 < heads:
                following = score(head + 1)
            lanes = pl.ds(head * HEAD_SIZE, HEAD_SIZE)
            old_top = top_ref[rows, lanes]
            top = jnp.maximum(old_top, jnp.max(scores, axis=1, keepdims=True) * LOG_SCALE)
            weights = jnp.exp2(scores * LOG_SCALE - top[:, :1]).astype(BF16)
            sums = jnp.dot(weights, wide_ref[...], preferred_element_type=F32)
            factor = jnp.exp2(old_top - top)
            top_ref[rows, lanes] = top
            part_ref[rows, lanes] = part_ref[rows, lanes] * factor + sums[:, :HEAD_SIZE]
            total_ref[rows, lanes] = total_ref[rows, lanes] * factor + sums[:, HEAD_SIZE:]
        return 0

    lax.fori_loop(0, 2, rows_step, 0)


def causal_step(mirrored, q_ref, key_ref, wide_ref, state):
    top_ref, total_ref, part_ref = state
    tokens = q_ref.shape[0]
    heads = q_ref.shape[1] // HEAD_SIZE
    chunk = tokens // HALF
    order = lax.broadcasted_iota(jnp.int32, (chunk, chunk), 0)
    allowed = order >= lax.broadcasted_iota(jnp.int32, (chunk, chunk), 1)
    for turn in range(HALF):
        start = jnp.where(mirrored == 1, (HALF - 1 - turn) * chunk, turn * chunk)
        rows = pl.ds(pl.multiple_of(start, chunk), chunk)
        if turn:
            earlier = jnp.where(mirrored == 1, (HALF - turn) * chunk, 0)
            before = pl.ds(pl.multiple_of(earlier, chunk), turn * chunk)
        for head in range(heads):
            lanes = pl.ds(head * HEAD_SIZE, HEAD_SIZE)
            query = q_ref[rows, lanes]
            near = jnp.where(allowed, scores_of(query, key_ref[rows, :]), EMPTY)
            top = jnp.max(near, axis=1, keepdims=True)
            if turn:
                far = scores_of(query, key_ref[before, :])
                top = jnp.maximum(top, jnp.max(far, axis=1, keepdims=True))
            top = top * LOG_SCALE
            weights = jnp.exp2(near * LOG_SCALE - top).astype(BF16)
            sums = jnp.dot(weights, wide_ref[rows, :], preferred_element_type=F32)
            if turn:
                weights = jnp.exp2(far * LOG_SCALE - top).astype(BF16)
                sums += jnp.dot(weights, wide_ref[before, :], preferred_element_type=F32)
            top_ref[rows, lanes] = jnp.broadcast_to(top, (chunk, HEAD_SIZE))
            part_ref[rows, lanes] = sums[:, :HEAD_SIZE]
            total_ref[rows, lanes] = sums[:, HEAD_SIZE:]


def start_sources(plan_ref, sources, buffer, sem):
    tokens = buffer.shape[0] // 3
    slot = jnp.int32(0)
    for column in range(3):
        here = jnp.bool_(False)
        for kind, pieces in sources.items():
            chosen = plan_ref[column] == kind
            here = here | chosen

            @pl.when(chosen)
            def _():
                begin = 0
                for number, ref in enumerate(pieces):
                    rows = pl.ds(pl.multiple_of(slot * tokens, tokens) + begin, ref.shape[0])
                    pltpu.make_async_copy(ref, buffer.at[rows], sem).start()
                    begin += ref.shape[0]

        slot = slot + here.astype(jnp.int32)
    return slot


def earlier_blocks(found, q_ref, wide_ref, buffer, sem, state):
    tokens = buffer.shape[0] // 3
    for number in (1, 2, 3):

        @pl.when(found == number)
        def _():
            here = buffer.at[pl.ds(0, number * tokens)]
            pltpu.make_async_copy(here, here, sem).wait()

    def add(rows):
        here, wide = buffer.at[rows], wide_ref.at[pl.ds(0, rows.size)]
        wide[:, :HEAD_SIZE] = here[:, HEAD_SIZE:]
        block_step(q_ref, here.at[:, pl.ds(0, HEAD_SIZE)], wide, state)

    pl.when(found >= 2)(lambda: add(pl.ds(0, 2 * tokens)))
    odd = pl.multiple_of((found // 2) * 2 * tokens, tokens)
    pl.when(found % 2 == 1)(lambda: add(pl.ds(odd, tokens)))


def attend_kernel(plan_ref, q_ref, *refs, pieces, first, last):
    refs = list(refs)

    def take(count):
        taken, refs[:] = refs[:count], refs[count:]
        return taken

    own_ref = take(1)[0] if first else None
    sources = {kind: take(count) for kind, count in pieces}
    old = [] if first else take(2)
    if last:
        (out_ref,) = take(1)
        (new_part,) = take(1)
    else:
        rows_out, new_part = take(2)
    top_ref, total_ref, wide_ref, buffer, sem = take(5)
    state = (top_ref, total_ref, new_part)
    found = start_sources(plan_ref, sources, buffer, sem)
    wide_ref[:, HEAD_SIZE:] = jnp.ones((wide_ref.shape[0], HEAD_SIZE), BF16)
    if first:
        wide = wide_ref.at[pl.ds(0, own_ref.shape[0])]
        wide[:, :HEAD_SIZE] = own_ref[:, HEAD_SIZE:]
        causal_step(plan_ref[3], q_ref, own_ref.at[:, pl.ds(0, HEAD_SIZE)], wide, state)
    else:
        rows_buffer, part_buffer, old_sem = refs
        copies = [
            pltpu.make_async_copy(old[0], rows_buffer, old_sem.at[0]),
            pltpu.make_async_copy(old[1], part_buffer, old_sem.at[1]),
        ]
        for copy in copies:
            copy.start()
        top_ref[...] = jnp.full(top_ref.shape, EMPTY, F32)
        total_ref[...] = jnp.zeros(total_ref.shape, F32)
        new_part[...] = jnp.zeros(new_part.shape, F32)
    earlier_blocks(found, q_ref, wide_ref, buffer, sem, state)
    if not first:
        for copy in copies:
            copy.wait()
    heads = q_ref.shape[1] // HEAD_SIZE
    packed = jnp.zeros((q_ref.shape[0], HEAD_SIZE), F32)
    lane = lax.broadcasted_iota(jnp.int32, packed.shape, 1)
    for head in range(heads):
        lanes = pl.ds(head * HEAD_SIZE, HEAD_SIZE)
        top, total = top_ref[:, lanes], total_ref[:, lanes]
        if not first:
            old_top = rows_buffer[:, head : head + 1]
            old_total = rows_buffer[:, heads + head : heads + head + 1]
            both_top = jnp.maximum(old_top, top)
            before, now = jnp.exp2(old_top - both_top), jnp.exp2(top - both_top)
            top, total = both_top, old_total * before + total * now
            part = part_buffer[:, lanes] * before + new_part[:, lanes] * now
            if last:
                out_ref[:, lanes] = (part / total).astype(BF16)
            else:
                new_part[:, lanes] = part
        if not last:
            packed = jnp.where(lane == head, top, packed)
            packed = jnp.where(lane == heads + head, total, packed)
    if not last:
        rows_out[...] = packed


VMEM = pl.BlockSpec(memory_space=pltpu.VMEM)
SMEM = pl.BlockSpec(memory_space=pltpu.SMEM)
ANY = pl.BlockSpec(memory_space=pl.ANY)
PARAMS = dict(vmem_limit_bytes=40 * 2**20)


def attend(plan, query, blocks, own=None, state=None, last=False):
    tokens = query.shape[0]
    first = own is not None
    running, packed = (query.shape, F32), ((tokens, HEAD_SIZE), F32)
    result = [(query.shape, BF16)] if last else [packed, running]
    pieces = [piece for kind in blocks for piece in blocks[kind]]
    scratch = [pltpu.VMEM(*running)] * (3 if last else 2) + [
        pltpu.VMEM((2 * tokens, 2 * HEAD_SIZE), BF16),
        pltpu.VMEM((3 * tokens, 2 * HEAD_SIZE), BF16),
        pltpu.SemaphoreType.DMA,
    ]
    if not first:
        scratch += [pltpu.VMEM(*packed), pltpu.VMEM(*running), pltpu.SemaphoreType.DMA((2,))]
    counts = tuple((kind, len(blocks[kind])) for kind in blocks)
    found = pl.pallas_call(
        functools.partial(attend_kernel, pieces=counts, first=first, last=last),
        out_shape=[jax.ShapeDtypeStruct(*kind) for kind in result],
        in_specs=[SMEM, VMEM] + [VMEM] * first + [ANY] * (len(pieces) + 2 * (not first)),
        out_specs=[VMEM] * len(result),
        scratch_shapes=scratch,
        compiler_params=pltpu.CompilerParams(**PARAMS),
    )(plan, query, *([own] if first else []), *pieces, *([] if first else state))
    return found[0] if last else found


def pass_kernel(plan_ref, block_ref, out_ref):
    for number in range(plan_ref.shape[0]):
        out_ref[number] = plan_ref[number]


def passed(plan, block):
    return pl.pallas_call(
        pass_kernel,
        out_shape=jax.ShapeDtypeStruct(plan.shape, plan.dtype),
        in_specs=[SMEM, ANY],
        out_specs=SMEM,
        cost_estimate=pl.CostEstimate(flops=10000000000, bytes_accessed=1000000, transcendentals=0),
    )(plan, block)


CALLS = ((4, 8, 1), (2, 16), (32,))


def per_device(query_input, encoded_keys, input_values, sources):
    tokens = query_input.shape[0]
    span = lax.axis_index("seq")
    column = span % COLUMN
    mirrored = (span // COLUMN) % 2

    plan = jnp.where(sources[0] >= 0, span - sources[0], 0).astype(jnp.int32)
    plan = jnp.concatenate([plan, mirrored[None].astype(jnp.int32)])

    def slots(value):
        return value.reshape(tokens, SLOTS, -1)

    both = jnp.concatenate([slots(encoded_keys), slots(input_values)], 2).transpose(1, 0, 2)
    own = exchange(both).reshape(-1, 2 * HEAD_SIZE)
    query_cut = slots(query_input).transpose(1, 0, 2)
    four = moved(own, ahead(4))
    eight = moved(own, ahead(8))
    query = exchange(query_cut).reshape(tokens * SLOTS, -1)
    blocks = {
        1: moved(jnp.where(column >= 3, four, own), along_row(1)),
        2: moved(jnp.where(column >= 2, four, own), along_row(2)),
        4: four,
        8: eight,
        16: moved(eight, ahead(8)),
        32: moved(moved(own, behind(0, 1, 2, 3)), behind(6, 7, 0, 1)),
    }
    blocks = {kind: [blocks[kind]] for kind in blocks}
    plan = passed(plan, blocks[1][0])
    state = None
    for number, kinds in enumerate(CALLS):
        state = attend(
            plan,
            query,
            {kind: blocks[kind] for kind in kinds},
            own=own if number == 0 else None,
            state=state,
            last=number == len(CALLS) - 1,
        )
    back = exchange(state.reshape(SLOTS, tokens, -1))
    return back.transpose(1, 0, 2).reshape(tokens, -1)


def solution(mesh):
    in_specs = (P(AXES, None), P(AXES, None), P(AXES, None), P("seq", None))
    return jax.shard_map(
        per_device, mesh=mesh, in_specs=in_specs, out_specs=P(AXES, None), check_vma=False
    )
```

```python
import functools

import jax
import jax.numpy as jnp
import numpy as np
from jax import lax
from jax.experimental import pallas as pl
from jax.experimental.pallas import tpu as pltpu
from jax.sharding import PartitionSpec as P

HEAD_SIZE = 128
AXES = ("seq", "head")
SPANS, SLOTS, HALF, COLUMN, PLANE = 64, 8, 4, 4, 8
LOG_SCALE = float(HEAD_SIZE**-0.5 * np.log2(np.e))
EMPTY = -1e30
F32, BF16 = jnp.float32, jnp.bfloat16


def slot_order(span):
    if (span // COLUMN) % 2 == 0:
        return list(range(SLOTS))
    return [(SLOTS // 2 - 1 - slot // 2) * 2 + slot % 2 for slot in range(SLOTS)]


def exchange(value):
    groups = [[span * SLOTS + slot for slot in slot_order(span)] for span in range(SPANS)]
    return lax.all_to_all(
        value, AXES, split_axis=0, concat_axis=0, tiled=True, axis_index_groups=groups
    )


def moved(value, target):
    pairs = []
    for span in range(SPANS):
        goal = target(span)
        if goal is not None:
            here, there = slot_order(span), slot_order(goal)
            pairs += [(span * SLOTS + a, goal * SLOTS + b) for a, b in zip(here, there)]
    return lax.ppermute(value, AXES, pairs)


def ahead(distance):
    return lambda span: span + distance if span + distance < SPANS else None


def along_row(distance):
    return lambda span: span // COLUMN * COLUMN + (span + distance) % COLUMN


def behind(*planes):
    count = SPANS // PLANE

    def target(span):
        plane = span // PLANE
        return (plane - 2) % count * PLANE + span % PLANE if plane in planes else None

    return target


def scores_of(query, key):
    return lax.dot_general(query, key, (((1,), (1,)), ((), ())), preferred_element_type=F32)


def block_step(q_ref, key_ref, wide_ref, state):
    top_ref, total_ref, part_ref = state
    heads = q_ref.shape[1] // HEAD_SIZE
    half = q_ref.shape[0] // 2

    def rows_step(tile, _):
        rows = pl.ds(pl.multiple_of(tile * half, half), half)

        def score(head):
            return scores_of(q_ref[rows, pl.ds(head * HEAD_SIZE, HEAD_SIZE)], key_ref[...])

        following = score(0)
        for head in range(heads):
            scores = following
            if head + 1 < heads:
                following = score(head + 1)
            lanes = pl.ds(head * HEAD_SIZE, HEAD_SIZE)
            old_top = top_ref[rows, lanes]
            top = jnp.maximum(old_top, jnp.max(scores, axis=1, keepdims=True) * LOG_SCALE)
            weights = jnp.exp2(scores * LOG_SCALE - top[:, :1]).astype(BF16)
            sums = jnp.dot(weights, wide_ref[...], preferred_element_type=F32)
            factor = jnp.exp2(old_top - top)
            top_ref[rows, lanes] = top
            part_ref[rows, lanes] = part_ref[rows, lanes] * factor + sums[:, :HEAD_SIZE]
            total_ref[rows, lanes] = total_ref[rows, lanes] * factor + sums[:, HEAD_SIZE:]
        return 0

    lax.fori_loop(0, 2, rows_step, 0)


def causal_step(mirrored, q_ref, key_ref, wide_ref, state):
    top_ref, total_ref, part_ref = state
    tokens = q_ref.shape[0]
    heads = q_ref.shape[1] // HEAD_SIZE
    chunk = tokens // HALF
    order = lax.broadcasted_iota(jnp.int32, (chunk, chunk), 0)
    allowed = order >= lax.broadcasted_iota(jnp.int32, (chunk, chunk), 1)
    for turn in range(HALF):
        start = jnp.where(mirrored == 1, (HALF - 1 - turn) * chunk, turn * chunk)
        rows = pl.ds(pl.multiple_of(start, chunk), chunk)
        if turn:
            earlier = jnp.where(mirrored == 1, (HALF - turn) * chunk, 0)
            before = pl.ds(pl.multiple_of(earlier, chunk), turn * chunk)
        for head in range(heads):
            lanes = pl.ds(head * HEAD_SIZE, HEAD_SIZE)
            query = q_ref[rows, lanes]
            near = jnp.where(allowed, scores_of(query, key_ref[rows, :]), EMPTY)
            top = jnp.max(near, axis=1, keepdims=True)
            if turn:
                far = scores_of(query, key_ref[before, :])
                top = jnp.maximum(top, jnp.max(far, axis=1, keepdims=True))
            top = top * LOG_SCALE
            weights = jnp.exp2(near * LOG_SCALE - top).astype(BF16)
            sums = jnp.dot(weights, wide_ref[rows, :], preferred_element_type=F32)
            if turn:
                weights = jnp.exp2(far * LOG_SCALE - top).astype(BF16)
                sums += jnp.dot(weights, wide_ref[before, :], preferred_element_type=F32)
            top_ref[rows, lanes] = jnp.broadcast_to(top, (chunk, HEAD_SIZE))
            part_ref[rows, lanes] = sums[:, :HEAD_SIZE]
            total_ref[rows, lanes] = sums[:, HEAD_SIZE:]


def start_sources(plan_ref, sources, buffer, sem):
    tokens = buffer.shape[0] // 3
    slot = jnp.int32(0)
    for column in range(3):
        here = jnp.bool_(False)
        for kind, pieces in sources.items():
            chosen = plan_ref[column] == kind
            here = here | chosen

            @pl.when(chosen)
            def _():
                begin = 0
                for number, ref in enumerate(pieces):
                    rows = pl.ds(pl.multiple_of(slot * tokens, tokens) + begin, ref.shape[0])
                    pltpu.make_async_copy(ref, buffer.at[rows], sem).start()
                    begin += ref.shape[0]

        slot = slot + here.astype(jnp.int32)
    return slot


def earlier_blocks(found, q_ref, wide_ref, buffer, sem, state):
    tokens = buffer.shape[0] // 3
    for number in (1, 2, 3):

        @pl.when(found == number)
        def _():
            here = buffer.at[pl.ds(0, number * tokens)]
            pltpu.make_async_copy(here, here, sem).wait()

    def add(rows):
        here, wide = buffer.at[rows], wide_ref.at[pl.ds(0, rows.size)]
        wide[:, :HEAD_SIZE] = here[:, HEAD_SIZE:]
        block_step(q_ref, here.at[:, pl.ds(0, HEAD_SIZE)], wide, state)

    pl.when(found >= 2)(lambda: add(pl.ds(0, 2 * tokens)))
    odd = pl.multiple_of((found // 2) * 2 * tokens, tokens)
    pl.when(found % 2 == 1)(lambda: add(pl.ds(odd, tokens)))


def attend_kernel(plan_ref, q_ref, *refs, pieces, first, last):
    refs = list(refs)

    def take(count):
        taken, refs[:] = refs[:count], refs[count:]
        return taken

    own_ref = take(1)[0] if first else None
    sources = {kind: take(count) for kind, count in pieces}
    old = [] if first else take(2)
    if last:
        (out_ref,) = take(1)
        (new_part,) = take(1)
    else:
        rows_out, new_part = take(2)
    top_ref, total_ref, wide_ref, buffer, sem = take(5)
    state = (top_ref, total_ref, new_part)
    found = start_sources(plan_ref, sources, buffer, sem)
    wide_ref[:, HEAD_SIZE:] = jnp.ones((wide_ref.shape[0], HEAD_SIZE), BF16)
    if first:
        wide = wide_ref.at[pl.ds(0, own_ref.shape[0])]
        wide[:, :HEAD_SIZE] = own_ref[:, HEAD_SIZE:]
        causal_step(plan_ref[3], q_ref, own_ref.at[:, pl.ds(0, HEAD_SIZE)], wide, state)
    else:
        rows_buffer, part_buffer, old_sem = refs
        copies = [
            pltpu.make_async_copy(old[0], rows_buffer, old_sem.at[0]),
            pltpu.make_async_copy(old[1], part_buffer, old_sem.at[1]),
        ]
        for copy in copies:
            copy.start()
        top_ref[...] = jnp.full(top_ref.shape, EMPTY, F32)
        total_ref[...] = jnp.zeros(total_ref.shape, F32)
        new_part[...] = jnp.zeros(new_part.shape, F32)
    earlier_blocks(found, q_ref, wide_ref, buffer, sem, state)
    if not first:
        for copy in copies:
            copy.wait()
    heads = q_ref.shape[1] // HEAD_SIZE
    packed = jnp.zeros((q_ref.shape[0], HEAD_SIZE), F32)
    lane = lax.broadcasted_iota(jnp.int32, packed.shape, 1)
    for head in range(heads):
        lanes = pl.ds(head * HEAD_SIZE, HEAD_SIZE)
        top, total = top_ref[:, lanes], total_ref[:, lanes]
        if not first:
            old_top = rows_buffer[:, head : head + 1]
            old_total = rows_buffer[:, heads + head : heads + head + 1]
            both_top = jnp.maximum(old_top, top)
            before, now = jnp.exp2(old_top - both_top), jnp.exp2(top - both_top)
            top, total = both_top, old_total * before + total * now
            part = part_buffer[:, lanes] * before + new_part[:, lanes] * now
            if last:
                out_ref[:, lanes] = (part / total).astype(BF16)
            else:
                new_part[:, lanes] = part
        if not last:
            packed = jnp.where(lane == head, top, packed)
            packed = jnp.where(lane == heads + head, total, packed)
    if not last:
        rows_out[...] = packed


VMEM = pl.BlockSpec(memory_space=pltpu.VMEM)
SMEM = pl.BlockSpec(memory_space=pltpu.SMEM)
ANY = pl.BlockSpec(memory_space=pl.ANY)
PARAMS = dict(vmem_limit_bytes=40 * 2**20)


def attend(plan, query, blocks, own=None, state=None, last=False):
    tokens = query.shape[0]
    first = own is not None
    running, packed = (query.shape, F32), ((tokens, HEAD_SIZE), F32)
    result = [(query.shape, BF16)] if last else [packed, running]
    pieces = [piece for kind in blocks for piece in blocks[kind]]
    scratch = [pltpu.VMEM(*running)] * (3 if last else 2) + [
        pltpu.VMEM((2 * tokens, 2 * HEAD_SIZE), BF16),
        pltpu.VMEM((3 * tokens, 2 * HEAD_SIZE), BF16),
        pltpu.SemaphoreType.DMA,
    ]
    if not first:
        scratch += [pltpu.VMEM(*packed), pltpu.VMEM(*running), pltpu.SemaphoreType.DMA((2,))]
    counts = tuple((kind, len(blocks[kind])) for kind in blocks)
    found = pl.pallas_call(
        functools.partial(attend_kernel, pieces=counts, first=first, last=last),
        out_shape=[jax.ShapeDtypeStruct(*kind) for kind in result],
        in_specs=[SMEM, VMEM] + [VMEM] * first + [ANY] * (len(pieces) + 2 * (not first)),
        out_specs=[VMEM] * len(result),
        scratch_shapes=scratch,
        compiler_params=pltpu.CompilerParams(**PARAMS),
    )(plan, query, *([own] if first else []), *pieces, *([] if first else state))
    return found[0] if last else found


def pass_kernel(plan_ref, block_ref, out_ref):
    for number in range(plan_ref.shape[0]):
        out_ref[number] = plan_ref[number]


def passed(plan, block):
    return pl.pallas_call(
        pass_kernel,
        out_shape=jax.ShapeDtypeStruct(plan.shape, plan.dtype),
        in_specs=[SMEM, ANY],
        out_specs=SMEM,
        cost_estimate=pl.CostEstimate(flops=10000000000, bytes_accessed=1000000, transcendentals=0),
    )(plan, block)


CALLS = ((4, 8, 1), (2, 16, 32))


def per_device(query_input, encoded_keys, input_values, sources):
    tokens = query_input.shape[0]
    span = lax.axis_index("seq")
    column = span % COLUMN
    mirrored = (span // COLUMN) % 2

    plan = jnp.where(sources[0] >= 0, span - sources[0], 0).astype(jnp.int32)
    plan = jnp.concatenate([plan, mirrored[None].astype(jnp.int32)])

    def slots(value):
        return value.reshape(tokens, SLOTS, -1)

    both = jnp.concatenate([slots(encoded_keys), slots(input_values)], 2).transpose(1, 0, 2)
    own = exchange(both).reshape(-1, 2 * HEAD_SIZE)
    query_cut = slots(query_input).transpose(1, 0, 2)
    four = moved(own, ahead(4))
    eight = moved(own, ahead(8))
    query = exchange(query_cut).reshape(tokens * SLOTS, -1)
    blocks = {
        1: moved(jnp.where(column >= 3, four, own), along_row(1)),
        2: moved(jnp.where(column >= 2, four, own), along_row(2)),
        4: four,
        8: eight,
        16: moved(eight, ahead(8)),
        32: moved(moved(own, behind(0, 1, 2, 3)), behind(6, 7, 0, 1)),
    }
    blocks = {kind: [blocks[kind]] for kind in blocks}
    plan = passed(plan, blocks[1][0])
    state = None
    for number, kinds in enumerate(CALLS):
        state = attend(
            plan,
            query,
            {kind: blocks[kind] for kind in kinds},
            own=own if number == 0 else None,
            state=state,
            last=number == len(CALLS) - 1,
        )
    back = exchange(state.reshape(SLOTS, tokens, -1))
    return back.transpose(1, 0, 2).reshape(tokens, -1)


def solution(mesh):
    in_specs = (P(AXES, None), P(AXES, None), P(AXES, None), P("seq", None))
    return jax.shard_map(
        per_device, mesh=mesh, in_specs=in_specs, out_specs=P(AXES, None), check_vma=False
    )
```
